128 devices in a mesh: pp: 8 (over x_hi, y), tp: 16 (over x_lo, z, core).
Axes of the slice: x: 4 (x_hi: 2, x_lo: 2; x = x_hi * 2 + x_lo), y: 4, z: 4, core: 2. Of those that a mesh axis runs over, the one named last changes fastest.
Arguments:
- input_codes: bfloat16 [8, 256, 8192], P('pp', 'tp'), may hold values from -127 to 127
- input_exps: int32 [8, 64], P('pp'), may hold values from -7 to -4
- prefix_len: int32 [8], P('pp'), may hold values from 2048 to 8192, as said below
- norm_gain: bfloat16 [8, 8192], P('pp'), may hold values from 0.099609375 to 1.8984375
- w_query: bfloat16 [8, 8192, 8192], P('pp', None, 'tp'), may hold values from -0.0625 to 0.0625
- w_keyval: bfloat16 [8, 8192, 16, 256], P('pp', None, 'tp'), as said below
- w_out: bfloat16 [8, 8192, 8192], P('pp', 'tp'), may hold values from -1.5 to 1.5
- kv_cache: bfloat16 [8, 16, 8192, 256], P('pp', 'tp'), as said below
- partial_exps: int32 [8, 64], P('pp'), may hold values from -10 to -7
- share_exps: int32 [8, 64], P('pp'), may hold values from -2 to 0
- output_exps: int32 [8, 64], replicated, may hold values from -7 to -4
Outputs:
- received: bfloat16 [8, 256, 8192], P('pp', 'tp')
The draws below stay inside these ranges and needn't reach their ends.
Inputs may be any that keep to these rules, and one draw needn't show every extreme that they name: `prefix_len`: each section's length lies in 2048 to 8192, and some section has exactly 8192. `w_keyval`: along the third dimension, the 2 entries 2 * g to 2 * g + 1 are equal (one key and value head for them). `kv_cache`: along the second dimension, the 2 entries 2 * g to 2 * g + 1 are equal (one key and value head for them).
All inputs are finite; a program needn't handle non-finite values.
Results may differ from the reference program's by a relative error of at most 0.029.
The reference program's roundings to bfloat16 on the way count: a program that leaves them out, or rounds other values in their place, can miss the bound.
Values may be sent and summed in bfloat16 or wider, within the bound.
A program may use at most 128 MiB of HBM per device.

```python
import math
import jax
import jax.numpy as jnp
from jax import lax

D = 8192
QH = 64
KVH = 8
HD = 128
GROUP = 128
PREFIX = 8192
NEW_TOK = 256
SECTIONS = 8
GROUPS = 64
COPIES = 2
N_PP = 8
N_TP = 16


def draw_prefix_len(key, part):
    key = jax.random.fold_in(key, 11)
    first_key, second_key = jax.random.split(key)
    base = jax.random.randint(first_key, (SECTIONS,), PREFIX // 4, PREFIX + 1)
    picked = jax.random.randint(second_key, (), 0, SECTIONS)
    return jnp.where(jnp.arange(SECTIONS) == picked, PREFIX, base).astype(jnp.int32)


def draw_w_keyval(key, part):
    key = jax.random.fold_in(key, 12)
    base = jax.random.normal(key, (SECTIONS, D, KVH, 2 * HD), jnp.float32) * D ** (-0.5)
    return jnp.repeat(base, COPIES, axis=2).astype(jnp.bfloat16)


def draw_kv_cache(key, part):
    key = jax.random.fold_in(key, 13)
    base = jax.random.normal(key, (SECTIONS, KVH, PREFIX, 2 * HD), jnp.float32)
    return jnp.repeat(base, COPIES, axis=1).astype(jnp.bfloat16)


def touch_ends(drawn, key, least, high):
    longest = drawn.shape.index(max(drawn.shape))
    spots = []
    for shift in (0, 1):
        where = [jax.random.randint(jax.random.fold_in(key, axis), (), 0, length) for axis, length in enumerate(drawn.shape)]
        where[longest] = (where[longest] + shift) % drawn.shape[longest]
        spots.append(tuple(where))
    return drawn.at[spots[0]].set(least).at[spots[1]].set(high)


def level_of(rng, dims, cuts, low, largest):
    def one(axis_at, shards_of):
        steps = jax.random.uniform(jax.random.fold_in(jax.random.fold_in(rng, 6), axis_at), (shards_of,), jnp.float32, low / len(cuts), largest / len(cuts))
        return jnp.repeat(jnp.exp(steps), dims[axis_at] // shards_of).reshape((-1,) + (1,) * (len(dims) - axis_at - 1))

    loudness = one(*cuts[0])
    for cut in cuts[1:]:
        loudness = loudness * one(*cut)
    return loudness


def gaussian(rng, shape, deviation, reach, cuts=(), kind=jnp.bfloat16):
    entries = jax.random.normal(rng, shape, jnp.float32) * deviation
    if len(cuts) > 0:
        entries = level_of(rng, shape, cuts, -0.22, 0.18) * entries
    return jnp.clip(entries, min=-reach, max=reach).astype(kind)


def setup_inputs(seed: int = 0) -> dict:
    splits = jax.random.split(jax.random.key(seed), 12)
    input_codes = gaussian(splits[0], (SECTIONS, NEW_TOK, D), 40.0, 127.0, ((0, 8), (1, 16)))
    input_exps = touch_ends(jax.random.randint(splits[1], (SECTIONS, GROUPS), -7, -3), jax.random.fold_in(splits[1], 1), -7, (-3) - 1).astype(jnp.int32)
    prefix_len = draw_prefix_len(jax.random.fold_in(splits[11], 71), 0)
    norm_gain = jnp.clip(1.0 + 0.18 * jax.random.normal(splits[3], (SECTIONS, D), jnp.float32), 0.099609375, 1.8984375).astype(jnp.bfloat16)
    w_query = gaussian(splits[4], (SECTIONS, D, QH * HD), D ** -0.5, 0.0625, ((0, 8), (2, 16)))
    w_keyval = draw_w_keyval(jax.random.fold_in(splits[11], 71), 0)
    w_out = gaussian(splits[6], (SECTIONS, QH * HD, D), 16 ** -0.5, 1.5, ((0, 8), (1, 16)))
    kv_cache = draw_kv_cache(jax.random.fold_in(splits[11], 71), 0)
    partial_exps = touch_ends(jax.random.randint(splits[8], (SECTIONS, GROUPS), -10, -6), jax.random.fold_in(splits[8], 1), -10, (-6) - 1).astype(jnp.int32)
    share_exps = touch_ends(jax.random.randint(splits[9], (SECTIONS, GROUPS), -2, 1), jax.random.fold_in(splits[9], 1), -2, 0).astype(jnp.int32)
    output_exps = touch_ends(jax.random.randint(splits[10], (SECTIONS, GROUPS), -7, -3), jax.random.fold_in(splits[10], 1), -7, (-3) - 1).astype(jnp.int32)
    return {"input_codes": input_codes, "input_exps": input_exps, "prefix_len": prefix_len, "norm_gain": norm_gain, "w_query": w_query, "w_keyval": w_keyval, "w_out": w_out, "kv_cache": kv_cache, "partial_exps": partial_exps, "share_exps": share_exps, "output_exps": output_exps}


EPSILON = 1e-05
ROPE_BASE = 500000.0

def group_scale(exponents):
    return jnp.repeat(jnp.exp2(exponents.astype(jnp.float32)), GROUP)

def rope_tables(positions, head_dim):
    half_dim = head_dim // 2
    freqs = jnp.power(jnp.float32(ROPE_BASE), -2.0 * jnp.arange(half_dim, dtype=jnp.float32) / head_dim)
    angles = positions.astype(jnp.float32)[:, None] * freqs[None, :]
    return (jnp.cos(angles), jnp.sin(angles))

def apply_rotary(values, cosine, sine):
    half_dim = values.shape[-1] // 2
    first_half = values[..., :half_dim]
    second_half = values[..., half_dim:]
    return jnp.concatenate([first_half * cosine - second_half * sine, second_half * cosine + first_half * sine], axis=-1)

def attention(queries, new_keys, new_values, cache_keys, cache_values, length):
    total_rows, head_count, head_dim = queries.shape
    block_rows = min(total_rows, 256)
    scale = 1.0 / math.sqrt(head_dim)
    cache_live = jnp.arange(cache_keys.shape[0], dtype=jnp.int32) < length
    key_index = jnp.arange(total_rows, dtype=jnp.int32)
    blocks = queries.reshape(total_rows // block_rows, block_rows, head_count, head_dim)
    starts = jnp.arange(total_rows // block_rows, dtype=jnp.int32) * block_rows
    cache_keys32 = cache_keys.astype(jnp.float32)
    cache_values32 = cache_values.astype(jnp.float32)
    new_keys32 = new_keys.astype(jnp.float32)
    new_values32 = new_values.astype(jnp.float32)

    def one_block(pair):
        query_block, start = pair
        query_block = query_block.astype(jnp.float32)
        old_scores = jnp.einsum('qhd,kd->hqk', query_block, cache_keys32) * scale
        old_scores = jnp.where(cache_live[None, None, :], old_scores, -jnp.inf)
        query_index = start + jnp.arange(block_rows, dtype=jnp.int32)
        new_scores = jnp.einsum('qhd,kd->hqk', query_block, new_keys32) * scale
        new_scores = jnp.where(key_index[None, None, :] <= query_index[None, :, None], new_scores, -jnp.inf)
        highest = jnp.maximum(lax.optimization_barrier(jnp.max(old_scores, axis=-1, keepdims=True)), lax.optimization_barrier(jnp.max(new_scores, axis=-1, keepdims=True)))
        old_weights = jnp.exp(old_scores - highest)
        new_weights = jnp.exp(new_scores - highest)
        denominator = lax.optimization_barrier(jnp.sum(old_weights, axis=-1, keepdims=True)) + lax.optimization_barrier(jnp.sum(new_weights, axis=-1, keepdims=True))
        old_weights = (old_weights / denominator).astype(jnp.bfloat16).astype(jnp.float32)
        new_weights = (new_weights / denominator).astype(jnp.bfloat16).astype(jnp.float32)
        mixed = jnp.einsum('hqk,kd->qhd', old_weights, cache_values32) + jnp.einsum('hqk,kd->qhd', new_weights, new_values32)
        return mixed.astype(jnp.bfloat16)
    mixed = lax.map(one_block, (blocks, starts))
    return mixed.reshape(total_rows, head_count * head_dim)

def reference(input_codes, input_exps, prefix_len, norm_gain, w_query, w_keyval, w_out, kv_cache, partial_exps, share_exps, output_exps):
    per_group = QH // KVH
    head_cols = QH * HD // N_TP
    results = []
    for section in range(N_PP):
        resid = input_codes[section].astype(jnp.float32) * group_scale(input_exps[section])
        power = lax.optimization_barrier(jnp.mean(resid * resid, axis=-1, keepdims=True))
        normed = (resid * lax.rsqrt(power + EPSILON) * norm_gain[section].astype(jnp.float32)).astype(jnp.bfloat16)
        queries = jnp.dot(normed, w_query[section], preferred_element_type=jnp.float32)
        keyval_weight = w_keyval[section][:, ::COPIES, :].reshape(D, KVH * 2 * HD)
        keyvals = jnp.dot(normed, keyval_weight, preferred_element_type=jnp.float32).reshape(NEW_TOK, KVH, 2 * HD)
        length = prefix_len[section]
        positions = length + jnp.arange(NEW_TOK, dtype=jnp.int32)
        cosine, sine = rope_tables(positions, HD)
        rot_query = apply_rotary(queries.reshape(NEW_TOK, QH, HD), cosine[:, None, :], sine[:, None, :]).astype(jnp.bfloat16)
        new_keys = apply_rotary(keyvals[:, :, :HD], cosine[:, None, :], sine[:, None, :]).astype(jnp.bfloat16)
        new_values = keyvals[:, :, HD:].astype(jnp.bfloat16)
        cache = kv_cache[section][::COPIES]
        grouped = jnp.transpose(rot_query.reshape(NEW_TOK, KVH, per_group, HD), (1, 0, 2, 3))

        def group_attention(items):
            query_group, keys_group, values_group, cache_group = items
            return attention(query_group, keys_group, values_group, cache_group[:, :HD], cache_group[:, HD:], length)
        mixed = lax.map(group_attention, (grouped, jnp.transpose(new_keys, (1, 0, 2)), jnp.transpose(new_values, (1, 0, 2)), cache))
        attended = jnp.transpose(mixed, (1, 0, 2)).reshape(NEW_TOK, QH * HD)
        inverse_part = group_scale(-partial_exps[section])
        out_weight = w_out[section]

        def add_term(total, rank):
            begin = (rank * head_cols).astype(jnp.int32)
            cols = lax.dynamic_slice_in_dim(attended, begin, head_cols, 1)
            rows = lax.dynamic_slice_in_dim(out_weight, begin, head_cols, 0)
            partial_value = jnp.dot(cols, rows, preferred_element_type=jnp.float32)
            codes = jnp.clip(partial_value * inverse_part, -127.0, 127.0).astype(jnp.bfloat16)
            codes = lax.optimization_barrier(codes)
            return (total + codes.astype(jnp.float32), None)
        total, _ = lax.scan(add_term, jnp.zeros((NEW_TOK, D), jnp.float32), jnp.arange(N_TP, dtype=jnp.int32))
        summed = total * group_scale(partial_exps[section])
        codes4 = jnp.clip(summed * group_scale(-share_exps[section]), -7.0, 7.0).astype(jnp.bfloat16)
        codes4 = lax.optimization_barrier(codes4)
        updated = resid + codes4.astype(jnp.float32) * group_scale(share_exps[section])
        out_codes = jnp.clip(updated * group_scale(-output_exps[section]), -127.0, 127.0).astype(jnp.bfloat16)
        out_codes = lax.optimization_barrier(out_codes)
        results.append((out_codes.astype(jnp.float32) * group_scale(output_exps[section])).astype(jnp.bfloat16))
    return jnp.roll(jnp.stack(results), 1, axis=0)
```

```python
import functools
import math

import jax
import jax.numpy as jnp
import numpy as np
from jax import lax
from jax.experimental import pallas as pl
from jax.experimental.pallas import tpu as pltpu
from jax.sharding import PartitionSpec as P

EPSILON = 1e-05
ROPE_BASE = 500000.0
MESH = pl.DeviceIdType.MESH
BF = jnp.bfloat16
F32 = jnp.float32

SECTIONS = 8
D = 8192
HD = 128
HEADS = 4
ROWS = 16
BLOCK = 128
TOKENS = 256
PREFIX = 8192
LEAST = 2048
KC = 1024
NK = D // KC
HALF = D // 2
JC = 1024
NJ = HALF // JC
KEYS = 1024

AG_SEMS = 14
RS_SEMS = 8


def dot(a, b):
    return jnp.dot(a, b, preferred_element_type=F32)


def dot_t(a, b):
    return lax.dot_general(a, b, (((1,), (1,)), ((), ())), preferred_element_type=F32)


def token_of(row):
    return (((row % BLOCK) // ROWS) * 2 + row // BLOCK) * ROWS + row % ROWS


def kernel(
    codes,
    in_exps,
    prefix_len,
    gain,
    freqs,
    wq_hbm,
    wkv_hbm,
    wo_hbm,
    kv_hbm,
    part_exps,
    share_exps,
    out_exps,
    out,
    gathered,
    wq,
    wkv,
    wo,
    kv,
    keys,
    tables,
    acc,
    cosine,
    sine,
    queries,
    new_keys,
    new_values,
    attended,
    partial,
    from_sib,
    sums,
    from_x,
    from_z1,
    from_z2,
    outgoing,
    sib_codes,
    load_sem,
    ag_send,
    ag_recv,
    rs_send,
    rs_recv,
    code_sem,
    pp_send,
    pp_recv,
):
    section = lax.axis_index("pp")
    rank = lax.axis_index("tp")
    core = rank % 2
    z = (rank // 2) % 4
    x = rank // 8
    other = 1 - core
    ox = 1 - x
    zn = (z + 1) % 4
    zp = (z + 3) % 4
    zo = (z + 2) % 4

    def device(xx, zz, cc, steps=0):
        return {"pp": (section + steps) % SECTIONS, "tp": (xx * 4 + zz) * 2 + cc}

    to_next = device(x, zn, core)
    to_prev = device(x, zp, core)
    to_x = device(ox, z, core)
    to_sib = device(x, z, other)

    barrier = pltpu.get_barrier_semaphore()
    greeted = [to_next, to_prev, to_x, to_sib]
    for steps in (1, SECTIONS - 1):
        for cc in (core, other):
            greeted.append(device(x, z, cc, steps))
    for peer in greeted:
        pl.semaphore_signal(barrier, inc=1, device_id=peer, device_id_type=MESH)

    loads = [
        pltpu.make_async_copy(src, dst, load_sem.at[i])
        for i, (src, dst) in enumerate(
            ((wq_hbm, wq), (wkv_hbm, wkv), (kv_hbm, kv), (wo_hbm, wo))
        )
    ]
    for load in loads:
        load.start()

    @pl.loop(0, D // HD // 8)
    def _(chunk):
        for inner in range(8):
            group = chunk * 8 + inner
            cols = pl.ds(pl.multiple_of(group * HD, HD), HD)

            def put(row, exponent):
                value = jnp.full((1, HD), jnp.left_shift(1, exponent + 16), jnp.int32)
                tables[row : row + 1, cols] = value.astype(F32) * (2.0**-16)

            part = part_exps[0, group]
            share = share_exps[0, group]
            outer = out_exps[section, group]
            put(0, in_exps[0, group])
            put(1, -part)
            put(2, part - share)
            put(3, share)
            put(4, -outer)
            put(5, outer)

    own_row = pl.multiple_of(core * BLOCK + (x * 4 + z) * ROWS, ROWS)
    power = jnp.zeros((ROWS, 1), F32)
    for k in range(NK):
        cols = slice(k * KC, (k + 1) * KC)
        resid = codes[:, cols].astype(F32) * tables[0:1, cols]
        power = power + jnp.sum(resid * resid, axis=1, keepdims=True)
    inverse = lax.rsqrt(power * (1.0 / D) + EPSILON)
    for k in range(NK):
        cols = slice(k * KC, (k + 1) * KC)
        resid = codes[:, cols].astype(F32) * tables[0:1, cols]
        gathered[k, pl.ds(own_row, ROWS), :] = (
            resid * inverse * gain[:, cols].astype(F32)
        ).astype(BF)

    pl.semaphore_wait(barrier, len(greeted))

    pending = []

    def remote(src, dst, send, recv, peer):
        copy = pltpu.make_async_remote_copy(
            src_ref=src,
            dst_ref=dst,
            send_sem=send,
            recv_sem=recv,
            device_id=peer,
            device_id_type=MESH,
        )
        copy.start()
        pending.append(copy)
        return copy

    sib_cols = pl.ds(pl.multiple_of(other * HALF, HALF), HALF)
    own_cols = pl.ds(pl.multiple_of(core * HALF, HALF), HALF)
    code_copy = remote(
        codes.at[:, sib_cols], sib_codes, code_sem.at[0], code_sem.at[1], to_sib
    )

    def piece(xx, zz):
        return pl.ds(pl.multiple_of(core * BLOCK + (xx * 4 + zz) * ROWS, ROWS), ROWS)

    full = slice(0, KC)
    low = slice(0, KC // 2)
    high = slice(KC // 2, KC)
    copies = {}

    def share(k, slot, rows, cols, peer):
        ref = gathered.at[k, rows, cols]
        copies[k, slot] = remote(ref, ref, ag_send.at[k, slot], ag_recv.at[k, slot], peer)

    def arrived(k, *slots):
        for slot in slots:
            copies[k, slot].wait_recv()

    def x_rows(xx):
        return pl.ds(pl.multiple_of(core * BLOCK + xx * (BLOCK // 2), BLOCK // 2), BLOCK // 2)

    def gather_stage(stage, k):
        z_first = k % 2 == 0
        if stage == 0:
            share(k, 0, piece(x, z), full, to_x)
            share(k, 1, piece(x, z), full, to_next)
            share(k, 2, piece(x, z), full, to_prev)
        elif z_first and stage == 1:
            arrived(k, 1, 2)
            share(k, 3, piece(x, zp), low, to_next)
            share(k, 4, piece(x, zn), high, to_prev)
            share(k, 5, piece(x, zp), full, to_x)
            share(k, 6, piece(x, zn), full, to_x)
        elif z_first and stage == 2:
            arrived(k, 3, 4)
            share(k, 7, piece(x, zo), full, to_x)
            share(k, 8, x_rows(x), full, to_sib)
        elif z_first and stage == 3:
            arrived(k, 0, 5, 6, 7)
            share(k, 9, x_rows(ox), full, to_sib)
        elif z_first and stage == 4:
            arrived(k, 8, 9)
        elif stage == 1:
            arrived(k, 0)
            share(k, 3, piece(ox, z), full, to_next)
            share(k, 4, piece(ox, z), full, to_prev)
        elif stage == 2:
            arrived(k, 1, 2, 3, 4)
            share(k, 5, piece(x, zp), low, to_next)
            share(k, 6, piece(ox, zp), low, to_next)
            share(k, 7, piece(x, zn), high, to_prev)
            share(k, 8, piece(ox, zn), high, to_prev)
        elif stage == 3:
            arrived(k, 5, 6, 7, 8)
            rows = pl.ds(pl.multiple_of(core * BLOCK, BLOCK), BLOCK)
            share(k, 9, rows, full, to_sib)
        else:
            arrived(k, 9)

    def project(k):
        rows = gathered[k]
        cols = slice(k * KC, (k + 1) * KC)
        if k == 0:
            acc[:, : HEADS * HD] = dot(rows, wq[cols, :])
            acc[:, HEADS * HD :] = dot(rows, wkv[cols, :])
        else:
            acc[:, : HEADS * HD] += dot(rows, wq[cols, :])
            acc[:, HEADS * HD :] += dot(rows, wkv[cols, :])

    length = prefix_len[0]

    def make_rotary():
        row = lax.broadcasted_iota(jnp.int32, (TOKENS, HD), 0)
        angle = (length + token_of(row)).astype(F32) * freqs[...]
        lane = lax.broadcasted_iota(jnp.int32, (TOKENS, HD), 1)
        cosine[...] = jnp.cos(angle)
        sine[...] = jnp.where(lane < HD // 2, -1.0, 1.0) * jnp.sin(angle)

    def make_keys():
        first = kv[0:ROWS, :HD][0:1, :]

        @pl.loop(0, PREFIX // 1024)
        def _(chunk):
            start = pl.multiple_of(chunk * 1024, 1024)
            rows = pl.ds(start, 1024)
            position = lax.broadcasted_iota(jnp.int32, (1024, HD), 0) + start
            live = position < length
            keys[rows, :] = jnp.where(live, kv[rows, :HD], first)
            kv[rows, HD:] = jnp.where(live, kv[rows, HD:], jnp.zeros((), BF))
            kv[rows, :HD] = jnp.where(live, 1.0, 0.0).astype(BF)

    LEAD = 2
    for tick in range(-LEAD, NK + 4):
        if tick + LEAD < NK:
            gather_stage(0, tick + LEAD)
        for stage in (1, 2, 3, 4):
            k = tick - stage + 1
            if 0 <= k < NK:
                gather_stage(stage, k)
        if tick == 0:
            make_rotary()
        if tick == 2:
            loads[2].wait()
            make_keys()
        if tick == 3:
            loads[0].wait()
            loads[1].wait()
        if 0 <= tick - 3 < NK:
            project(tick - 3)

    q_scale = math.log2(math.e) / math.sqrt(HD)

    def rotated(cols):
        value = acc[:, cols]
        return value * cosine[...] + pltpu.roll(value, HD // 2, 1) * sine[...]

    for head in range(HEADS):
        value = (rotated(slice(head * HD, (head + 1) * HD)) * q_scale).astype(BF)
        for block in range(2):
            queries[block, head * BLOCK : (head + 1) * BLOCK, :] = value[
                block * BLOCK : (block + 1) * BLOCK
            ]
    base = HEADS * HD
    new_keys[...] = rotated(slice(base, base + HD)).astype(BF)
    new_values[:, HD:] = acc[:, base + HD :].astype(BF)
    new_values[:, :HD] = jnp.ones((TOKENS, HD), BF)

    def attend(block, after):
        state = []
        row = lax.broadcasted_iota(jnp.int32, (BLOCK, TOKENS), 0) + block * BLOCK
        col = lax.broadcasted_iota(jnp.int32, (BLOCK, TOKENS), 1)
        seen = token_of(col) <= token_of(row)
        for head in range(HEADS):
            q = queries[block, head * BLOCK : (head + 1) * BLOCK, :]
            score = jnp.where(seen, dot_t(q, new_keys[...]), -1e30)
            top = jnp.max(score, axis=1, keepdims=True)
            weight = jnp.exp2(score - top).astype(BF)
            state.append((top, dot(weight, new_values[...])))
        for chunk in range(PREFIX // KEYS):
            rows = slice(chunk * KEYS, (chunk + 1) * KEYS)
            for head in range(HEADS):
                top, total = state[head]
                q = queries[block, head * BLOCK : (head + 1) * BLOCK, :]
                score = dot_t(q, keys[rows, :])
                new_top = jnp.maximum(top, jnp.max(score, axis=1, keepdims=True))
                weight = jnp.exp2(score - new_top).astype(BF)
                total = total * jnp.exp2(top - new_top) + dot(weight, kv[rows, :])
                state[head] = (new_top, total)
            after(chunk)
        for head in range(HEADS):
            total = state[head][1]
            attended[block, :, head * HD : (head + 1) * HD] = (
                total[:, HD:] / total[:, :HD]
            ).astype(BF)

    def half_cols(which, j):
        return pl.ds(pl.multiple_of(which * HALF + j * JC, JC), JC)

    def out_project(block, which, j):
        cols = half_cols(which, j)
        value = dot(attended[block], wo[:, cols]) * tables[1:2, cols]
        return jnp.clip(value, -127.0, 127.0).astype(BF)

    rs = {}

    def hand(block, j, slot, src, dst, peer):
        sem = block * NJ + j
        rs[block, j, slot] = remote(src, dst, rs_send.at[sem, slot], rs_recv.at[sem, slot], peer)

    def got(block, j, *slots):
        for slot in slots:
            rs[block, j, slot].wait_recv()

    def z_rows(zz):
        return pl.ds(pl.multiple_of(zz * ROWS, ROWS), ROWS)

    lo = slice(0, JC // 2)
    hi = slice(JC // 2, JC)

    def add(*values):
        total = values[0].astype(F32)
        for value in values[1:]:
            total = total + value.astype(F32)
        return total

    def produce(block, j):
        partial[block, j] = out_project(block, other, j)
        hand(block, j, 0, partial.at[block, j], from_sib.at[block, j], to_sib)
        sums[block, j] = out_project(block, core, j).reshape(2, BLOCK // 2, JC)

    def finish(block, j, total):
        cols = half_cols(core, j)
        is_own = core == block
        own = codes[:, cols]
        sib = sib_codes[:, j * JC : (j + 1) * JC]
        resid = jnp.where(is_own, own.astype(F32), sib.astype(F32)) * row_scale(block, cols)
        codes4 = jnp.clip(total * tables[2:3, cols], -7.0, 7.0).astype(BF)
        updated = resid + codes4.astype(F32) * tables[3:4, cols]
        coded = jnp.clip(updated * tables[4:5, cols], -127.0, 127.0).astype(BF)
        outgoing[block, j] = (coded.astype(F32) * tables[5:6, cols]).astype(BF)
        slot = core * NJ + j
        remote(
            outgoing.at[block, j],
            out.at[:, cols],
            pp_send.at[block, j],
            pp_recv.at[slot],
            device(x, z, block, 1),
        )

    def row_scale(block, cols):
        return tables[0:1, cols]

    def reduce_stage(stage, block, j):
        ref = sums.at[block, j]
        z_first = j >= NJ // 2
        if stage == 0:
            got(block, j, 0)
            for part in range(2):
                rows = slice(part * (BLOCK // 2), (part + 1) * (BLOCK // 2))
                ref[part] = add(ref[part], from_sib[block, j, rows, :]).astype(BF)
            if z_first:
                hand(block, j, 1, ref.at[:, z_rows(zo), lo], from_z1.at[block, j, 0], to_next)
                hand(block, j, 2, ref.at[:, z_rows(zo), hi], from_z1.at[block, j, 1], to_prev)
            else:
                hand(block, j, 1, ref.at[ox], from_x.at[block, j], to_x)
        elif z_first and stage == 1:
            got(block, j, 1, 2)
            ref[:, z_rows(zn), lo] = add(ref[:, z_rows(zn), lo], from_z1[block, j, 0]).astype(BF)
            ref[:, z_rows(zp), hi] = add(ref[:, z_rows(zp), hi], from_z1[block, j, 1]).astype(BF)
            hand(block, j, 3, ref.at[:, z_rows(zn), :], from_z2.at[block, j, 0], to_next)
            hand(block, j, 4, ref.at[:, z_rows(zp), :], from_z2.at[block, j, 1], to_prev)
        elif z_first and stage == 2:
            got(block, j, 3, 4)
            ref[:, z_rows(z), :] = add(
                ref[:, z_rows(z), :], from_z2[block, j, 0], from_z2[block, j, 1]
            ).astype(BF)
            hand(
                block,
                j,
                5,
                ref.at[ox, z_rows(z), :],
                from_x.at[block, j, 0:ROWS, :],
                to_x,
            )
        elif z_first:
            got(block, j, 5)
            finish(block, j, add(ref[x, z_rows(z), :], from_x[block, j, 0:ROWS, :]))
        elif stage == 1:
            got(block, j, 1)
            ref[x] = add(ref[x], from_x[block, j]).astype(BF)
            hand(block, j, 2, ref.at[x, z_rows(zo), lo], from_z1.at[block, j, 0, 0], to_next)
            hand(block, j, 3, ref.at[x, z_rows(zo), hi], from_z1.at[block, j, 1, 0], to_prev)
        elif stage == 2:
            got(block, j, 2, 3)
            ref[x, z_rows(zn), lo] = add(ref[x, z_rows(zn), lo], from_z1[block, j, 0, 0]).astype(BF)
            ref[x, z_rows(zp), hi] = add(ref[x, z_rows(zp), hi], from_z1[block, j, 1, 0]).astype(BF)
            hand(block, j, 4, ref.at[x, z_rows(zn), :], from_z2.at[block, j, 0, 0], to_next)
            hand(block, j, 5, ref.at[x, z_rows(zp), :], from_z2.at[block, j, 1, 0], to_prev)
        else:
            got(block, j, 4, 5)
            finish(
                block,
                j,
                add(ref[x, z_rows(z), :], from_z2[block, j, 0, 0], from_z2[block, j, 1, 0]),
            )

    code_copy.wait_recv()
    attend(0, lambda chunk: None)
    loads[3].wait()

    def steps_of(block):
        return [(0, 2), (1, 2), (0, 3), (1, 3), (2, 2), (1, 0), (2, 3), (3, 2), (1, 1), (2, 0), (3, 3), (2, 1), (3, 0), (3, 1)]

    def run_produce(block):
        for j in range(NJ):
            produce(block, j)
            if j >= 1:
                if j - 1 < NJ // 2:
                    reduce_stage(0, block, j - 1)

    run_produce(0)
    todo = [(stage, 0, j) for stage, j in steps_of(0)]

    def serve(chunk):
        for _ in range(2):
            if todo:
                reduce_stage(*todo.pop(0))

    attend(1, serve)
    run_produce(1)
    for item in todo:
        reduce_stage(*item)
    for stage, j in steps_of(1):
        reduce_stage(stage, 1, j)

    for which in range(2):
        for j in range(NJ):
            ref = out.at[:, pl.ds(which * HALF + j * JC, JC)]
            pltpu.make_async_copy(ref, ref, pp_recv.at[which * NJ + j]).wait()
    for copy in pending:
        copy.wait_send()


def local(
    input_codes,
    input_exps,
    prefix_len,
    norm_gain,
    w_query,
    w_keyval,
    w_out,
    kv_cache,
    partial_exps,
    share_exps,
    output_exps,
):
    half = np.power(np.float64(ROPE_BASE), -2.0 * np.arange(HD // 2) / HD).astype(np.float32)
    freqs = jnp.asarray(np.concatenate([half, half])[None, :])
    vmem = pl.BlockSpec(memory_space=pltpu.VMEM)
    smem = pl.BlockSpec(memory_space=pltpu.SMEM)
    hbm = pl.BlockSpec(memory_space=pl.ANY)
    dma = pltpu.SemaphoreType.DMA
    scratch = [
        pltpu.VMEM((NK, TOKENS, KC), BF),
        pltpu.VMEM((D, HEADS * HD), BF),
        pltpu.VMEM((D, 2 * HD), BF),
        pltpu.VMEM((HEADS * HD, D), BF),
        pltpu.VMEM((PREFIX, 2 * HD), BF),
        pltpu.VMEM((PREFIX, HD), BF),
        pltpu.VMEM((8, D), F32),
        pltpu.VMEM((TOKENS, (HEADS + 2) * HD), F32),
        pltpu.VMEM((TOKENS, HD), F32),
        pltpu.VMEM((TOKENS, HD), F32),
        pltpu.VMEM((2, HEADS * BLOCK, HD), BF),
        pltpu.VMEM((TOKENS, HD), BF),
        pltpu.VMEM((TOKENS, 2 * HD), BF),
        pltpu.VMEM((2, BLOCK, HEADS * HD), BF),
        pltpu.VMEM((2, NJ, BLOCK, JC), BF),
        pltpu.VMEM((2, NJ, BLOCK, JC), BF),
        pltpu.VMEM((2, NJ, 2, BLOCK // 2, JC), BF),
        pltpu.VMEM((2, NJ, BLOCK // 2, JC), BF),
        pltpu.VMEM((2, NJ, 2, 2, ROWS, JC // 2), BF),
        pltpu.VMEM((2, NJ, 2, 2, ROWS, JC), BF),
        pltpu.VMEM((2, NJ, ROWS, JC), BF),
        pltpu.VMEM((ROWS, HALF), BF),
        dma((4,)),
        dma((NK, 10)),
        dma((NK, 10)),
        dma((2 * NJ, 6)),
        dma((2 * NJ, 6)),
        dma((2,)),
        dma((2, NJ)),
        dma((2 * NJ,)),
    ]
    received = pl.pallas_call(
        kernel,
        out_shape=jax.ShapeDtypeStruct((ROWS, D), BF),
        in_specs=[vmem, smem, smem, vmem, vmem, hbm, hbm, hbm, hbm, smem, smem, smem],
        out_specs=hbm,
        scratch_shapes=scratch,
        compiler_params=pltpu.CompilerParams(
            collective_id=1, has_side_effects=True, vmem_limit_bytes=60 * 2**20
        ),
        cost_estimate=pl.CostEstimate(
            flops=10 * 10**9, bytes_accessed=26 * 2**20, transcendentals=9 * 10**6
        ),
        name="relay_section",
    )(
        input_codes[0],
        input_exps,
        prefix_len,
        norm_gain,
        freqs,
        w_query[0],
        w_keyval.reshape(D, 2 * HD),
        w_out[0],
        kv_cache.reshape(PREFIX, 2 * HD),
        partial_exps,
        share_exps,
        output_exps,
    )
    return received[None]


def solution(mesh):
    in_specs = (
        P("pp", "tp", None),
        P("pp", None),
        P("pp"),
        P("pp", None),
        P("pp", None, "tp"),
        P("pp", None, "tp", None),
        P("pp", "tp", None),
        P("pp", "tp", None, None),
        P("pp", None),
        P("pp", None),
        P(),
    )
    out_specs = P("pp", "tp", None)
    return jax.shard_map(local, mesh=mesh, in_specs=in_specs, out_specs=out_specs, check_vma=False)
```

```python
import functools
import math

import jax
import jax.numpy as jnp
import numpy as np
from jax import lax
from jax.experimental import pallas as pl
from jax.experimental.pallas import tpu as pltpu
from jax.sharding import PartitionSpec as P

EPSILON = 1e-05
ROPE_BASE = 500000.0
MESH = pl.DeviceIdType.MESH
BF = jnp.bfloat16
F32 = jnp.float32

SECTIONS = 8
D = 8192
HD = 128
HEADS = 4
ROWS = 16
BLOCK = 128
TOKENS = 256
PREFIX = 8192
LEAST = 2048
KC = 1024
NK = D // KC
HALF = D // 2
JC = 1024
NJ = HALF // JC
KEYS = 1024

Z_FIRST = "zxzxzxzx"
X_REDUCE = "xzxz"


def dot(a, b):
    return jnp.dot(a, b, preferred_element_type=F32)


def dot_t(a, b):
    return lax.dot_general(a, b, (((1,), (1,)), ((), ())), preferred_element_type=F32)


def token_of(row):
    return (((row % BLOCK) // ROWS) * 2 + row // BLOCK) * ROWS + row % ROWS


def kernel(
    codes,
    in_exps,
    prefix_len,
    gain,
    freqs,
    wq_hbm,
    wkv_hbm,
    wo_hbm,
    kv_hbm,
    part_exps,
    share_exps,
    out_exps,
    out,
    gathered,
    wq,
    wkv,
    wo,
    kv,
    keys,
    tables,
    acc,
    cosine,
    sine,
    queries,
    new_keys,
    new_values,
    attended,
    partial,
    from_sib,
    sums,
    from_x,
    from_z,
    outgoing,
    sib_codes,
    load_sem,
    ag_send,
    ag_recv,
    rs_send,
    rs_recv,
    code_sem,
    pp_send,
    pp_recv,
):
    section = lax.axis_index("pp")
    rank = lax.axis_index("tp")
    core = rank % 2
    z = (rank // 2) % 4
    x = rank // 8
    other = 1 - core
    ox = 1 - x
    zn = (z + 1) % 4
    zp = (z + 3) % 4
    zo = (z + 2) % 4

    def device(xx, zz, cc, steps=0):
        return {"pp": (section + steps) % SECTIONS, "tp": (xx * 4 + zz) * 2 + cc}

    to_next = device(x, zn, core)
    to_prev = device(x, zp, core)
    to_far = device(x, zo, core)
    to_x = device(ox, z, core)
    to_sib = device(x, z, other)

    barrier = pltpu.get_barrier_semaphore()
    greeted = [to_next, to_prev, to_far, to_x, to_sib]
    for cc in (core, other):
        greeted.append(device(x, z, cc, SECTIONS - 1))
    for peer in greeted:
        pl.semaphore_signal(barrier, inc=1, device_id=peer, device_id_type=MESH)

    loads = [
        pltpu.make_async_copy(src, dst, load_sem.at[i])
        for i, (src, dst) in enumerate(
            ((wq_hbm, wq), (wkv_hbm, wkv), (kv_hbm, kv), (wo_hbm, wo))
        )
    ]
    for load in loads:
        load.start()

    @pl.loop(0, D // HD // 8)
    def _(chunk):
        for inner in range(8):
            group = chunk * 8 + inner
            cols = pl.ds(pl.multiple_of(group * HD, HD), HD)

            def put(row, exponent):
                value = jnp.full((1, HD), jnp.left_shift(1, exponent + 16), jnp.int32)
                tables[row : row + 1, cols] = value.astype(F32) * (2.0**-16)

            part = part_exps[0, group]
            share = share_exps[0, group]
            outer = out_exps[section, group]
            put(0, in_exps[0, group])
            put(1, -part)
            put(2, part - share)
            put(3, share)
            put(4, -outer)
            put(5, outer)

    own_row = pl.multiple_of(core * BLOCK + (x * 4 + z) * ROWS, ROWS)
    power = jnp.zeros((ROWS, 1), F32)
    for k in range(NK):
        cols = slice(k * KC, (k + 1) * KC)
        resid = codes[:, cols].astype(F32) * tables[0:1, cols]
        power = power + jnp.sum(resid * resid, axis=1, keepdims=True)
    inverse = lax.rsqrt(power * (1.0 / D) + EPSILON)
    for k in range(NK):
        cols = slice(k * KC, (k + 1) * KC)
        resid = codes[:, cols].astype(F32) * tables[0:1, cols]
        gathered[k, pl.ds(own_row, ROWS), :] = (
            resid * inverse * gain[:, cols].astype(F32)
        ).astype(BF)

    pl.semaphore_wait(barrier, len(greeted))

    pending = []

    def remote(src, dst, send, recv, peer):
        copy = pltpu.make_async_remote_copy(
            src_ref=src,
            dst_ref=dst,
            send_sem=send,
            recv_sem=recv,
            device_id=peer,
            device_id_type=MESH,
        )
        copy.start()
        pending.append(copy)
        return copy

    sib_cols = pl.ds(pl.multiple_of(other * HALF, HALF), HALF)
    own_cols = pl.ds(pl.multiple_of(core * HALF, HALF), HALF)
    code_copy = remote(
        codes.at[:, sib_cols], sib_codes, code_sem.at[0], code_sem.at[1], to_sib
    )

    def piece(xx, zz):
        return pl.ds(pl.multiple_of(core * BLOCK + (xx * 4 + zz) * ROWS, ROWS), ROWS)

    full = slice(0, KC)
    low = slice(0, KC // 2)
    high = slice(KC // 2, KC)
    copies = {}

    def share(k, slot, rows, cols, peer):
        ref = gathered.at[k, rows, cols]
        copies[k, slot] = remote(ref, ref, ag_send.at[k, slot], ag_recv.at[k, slot], peer)

    def arrived(k, *slots):
        for slot in slots:
            copies[k, slot].wait_recv()

    def x_rows(xx):
        return pl.ds(pl.multiple_of(core * BLOCK + xx * (BLOCK // 2), BLOCK // 2), BLOCK // 2)

    def gather_stage(stage, k):
        z_first = Z_FIRST[k] == "z"
        if stage == 0:
            share(k, 0, piece(x, z), full, to_x)
            share(k, 1, piece(x, z), full, to_next)
            share(k, 2, piece(x, z), full, to_prev)
        elif z_first and stage == 1:
            arrived(k, 1, 2)
            share(k, 3, piece(x, zp), low, to_next)
            share(k, 4, piece(x, zn), high, to_prev)
            share(k, 5, piece(x, zp), full, to_x)
            share(k, 6, piece(x, zn), full, to_x)
        elif z_first and stage == 2:
            arrived(k, 3, 4)
            share(k, 7, piece(x, zo), full, to_x)
            share(k, 8, x_rows(x), full, to_sib)
        elif z_first and stage == 3:
            arrived(k, 0, 5, 6, 7)
            share(k, 9, x_rows(ox), full, to_sib)
        elif z_first and stage == 4:
            arrived(k, 8, 9)
        elif stage == 1:
            arrived(k, 0)
            share(k, 3, piece(ox, z), full, to_next)
            share(k, 4, piece(ox, z), full, to_prev)
        elif stage == 2:
            arrived(k, 1, 2, 3, 4)
            share(k, 5, piece(x, zp), low, to_next)
            share(k, 6, piece(ox, zp), low, to_next)
            share(k, 7, piece(x, zn), high, to_prev)
            share(k, 8, piece(ox, zn), high, to_prev)
        elif stage == 3:
            arrived(k, 5, 6, 7, 8)
            rows = pl.ds(pl.multiple_of(core * BLOCK, BLOCK), BLOCK)
            share(k, 9, rows, full, to_sib)
        else:
            arrived(k, 9)

    def project(k):
        rows = gathered[k]
        cols = slice(k * KC, (k + 1) * KC)
        if k == 0:
            acc[:, : HEADS * HD] = dot(rows, wq[cols, :])
            acc[:, HEADS * HD :] = dot(rows, wkv[cols, :])
        else:
            acc[:, : HEADS * HD] += dot(rows, wq[cols, :])
            acc[:, HEADS * HD :] += dot(rows, wkv[cols, :])

    length = prefix_len[0]

    def make_rotary():
        row = lax.broadcasted_iota(jnp.int32, (TOKENS, HD), 0)
        angle = (length + token_of(row)).astype(F32) * freqs[...]
        lane = lax.broadcasted_iota(jnp.int32, (TOKENS, HD), 1)
        cosine[...] = jnp.cos(angle)
        sine[...] = jnp.where(lane < HD // 2, -1.0, 1.0) * jnp.sin(angle)

    def make_keys():
        first = kv[0:ROWS, :HD][0:1, :]

        @pl.loop(0, PREFIX // 1024)
        def _(chunk):
            start = pl.multiple_of(chunk * 1024, 1024)
            rows = pl.ds(start, 1024)
            position = lax.broadcasted_iota(jnp.int32, (1024, HD), 0) + start
            live = position < length
            keys[rows, :] = jnp.where(live, kv[rows, :HD], first)
            kv[rows, HD:] = jnp.where(live, kv[rows, HD:], jnp.zeros((), BF))
            kv[rows, :HD] = jnp.where(live, 1.0, 0.0).astype(BF)

    for k in range(NK):
        gather_stage(0, k)
    make_rotary()
    for k in range(NK // 2):
        gather_stage(1, k)
    loads[2].wait()
    make_keys()
    for k in range(NK // 2, NK):
        gather_stage(1, k)
        gather_stage(2, k - NK // 2)
    loads[0].wait()
    loads[1].wait()
    for k in range(NK // 2, NK):
        gather_stage(2, k)
        gather_stage(3, k - NK // 2)
    for k in range(NK // 2, NK + 1):
        if k < NK:
            gather_stage(3, k)
        gather_stage(4, k - NK // 2)
        project(k - NK // 2)
    for k in range(NK // 2 + 1, NK):
        gather_stage(4, k)
        project(k)

    q_scale = math.log2(math.e) / math.sqrt(HD)

    def rotated(cols):
        value = acc[:, cols]
        return value * cosine[...] + pltpu.roll(value, HD // 2, 1) * sine[...]

    for head in range(HEADS):
        value = (rotated(slice(head * HD, (head + 1) * HD)) * q_scale).astype(BF)
        for block in range(2):
            queries[block, head * BLOCK : (head + 1) * BLOCK, :] = value[
                block * BLOCK : (block + 1) * BLOCK
            ]
    base = HEADS * HD
    new_keys[...] = rotated(slice(base, base + HD)).astype(BF)
    new_values[:, HD:] = acc[:, base + HD :].astype(BF)
    new_values[:, :HD] = jnp.ones((TOKENS, HD), BF)

    def attend(block, after):
        state = []
        row = lax.broadcasted_iota(jnp.int32, (BLOCK, TOKENS), 0) + block * BLOCK
        col = lax.broadcasted_iota(jnp.int32, (BLOCK, TOKENS), 1)
        seen = token_of(col) <= token_of(row)
        for head in range(HEADS):
            q = queries[block, head * BLOCK : (head + 1) * BLOCK, :]
            score = jnp.where(seen, dot_t(q, new_keys[...]), -1e30)
            top = jnp.max(score, axis=1, keepdims=True)
            weight = jnp.exp2(score - top).astype(BF)
            state.append((top, dot(weight, new_values[...])))
        for chunk in range(PREFIX // KEYS):
            rows = slice(chunk * KEYS, (chunk + 1) * KEYS)
            for head in range(HEADS):
                top, total = state[head]
                q = queries[block, head * BLOCK : (head + 1) * BLOCK, :]
                score = dot_t(q, keys[rows, :])
                new_top = jnp.maximum(top, jnp.max(score, axis=1, keepdims=True))
                weight = jnp.exp2(score - new_top).astype(BF)
                total = total * jnp.exp2(top - new_top) + dot(weight, kv[rows, :])
                state[head] = (new_top, total)
            after(chunk)
        for head in range(HEADS):
            total = state[head][1]
            attended[block, :, head * HD : (head + 1) * HD] = (
                total[:, HD:] / total[:, :HD]
            ).astype(BF)

    def half_cols(which, j):
        return pl.ds(pl.multiple_of(which * HALF + j * JC, JC), JC)

    def out_project(block, which, j):
        cols = half_cols(which, j)
        value = dot(attended[block], wo[:, cols]) * tables[1:2, cols]
        return jnp.clip(value, -127.0, 127.0).astype(BF)

    rs = {}

    def hand(block, j, slot, src, dst, peer):
        sem = block * NJ + j
        rs[block, j, slot] = remote(src, dst, rs_send.at[sem, slot], rs_recv.at[sem, slot], peer)

    def got(block, j, *slots):
        for slot in slots:
            rs[block, j, slot].wait_recv()

    def z_rows(zz):
        return pl.ds(pl.multiple_of(zz * ROWS, ROWS), ROWS)

    def add(*values):
        total = values[0].astype(F32)
        for value in values[1:]:
            total = total + value.astype(F32)
        return total

    def produce(block, j):
        partial[block, j] = out_project(block, other, j)
        hand(block, j, 0, partial.at[block, j], from_sib.at[block, j], to_sib)
        sums[block, j] = out_project(block, core, j).reshape(2, BLOCK // 2, JC)

    def finish(block, j, total):
        cols = half_cols(core, j)
        is_own = core == block
        own = codes[:, cols]
        sib = sib_codes[:, j * JC : (j + 1) * JC]
        resid = jnp.where(is_own, own.astype(F32), sib.astype(F32)) * row_scale(block, cols)
        codes4 = jnp.clip(total * tables[2:3, cols], -7.0, 7.0).astype(BF)
        updated = resid + codes4.astype(F32) * tables[3:4, cols]
        coded = jnp.clip(updated * tables[4:5, cols], -127.0, 127.0).astype(BF)
        outgoing[block, j] = (coded.astype(F32) * tables[5:6, cols]).astype(BF)
        slot = core * NJ + j
        remote(
            outgoing.at[block, j],
            out.at[:, cols],
            pp_send.at[block, j],
            pp_recv.at[slot],
            device(x, z, block, 1),
        )

    def row_scale(block, cols):
        return tables[0:1, cols]

    across = ((0, zn, to_next), (1, zp, to_prev), (2, zo, to_far))

    def reduce_stage(stage, block, j):
        ref = sums.at[block, j]
        x_first = X_REDUCE[j] == "x"
        if stage == 0:
            got(block, j, 0)
            for part in range(2):
                rows = slice(part * (BLOCK // 2), (part + 1) * (BLOCK // 2))
                ref[part] = add(ref[part], from_sib[block, j, rows, :]).astype(BF)
            if x_first:
                hand(block, j, 1, ref.at[ox], from_x.at[block, j], to_x)
            else:
                for slot, zz, peer in across:
                    hand(block, j, 1 + slot, ref.at[:, z_rows(zz), :], from_z.at[block, j, slot], peer)
        elif x_first and stage == 1:
            got(block, j, 1)
            ref[x] = add(ref[x], from_x[block, j]).astype(BF)
            for slot, zz, peer in across:
                hand(block, j, 2 + slot, ref.at[x, z_rows(zz), :], from_z.at[block, j, slot, 0], peer)
        elif x_first:
            got(block, j, 2, 3, 4)
            parts = [from_z[block, j, slot, 0] for slot in range(3)]
            finish(block, j, add(ref[x, z_rows(z), :], *parts))
        elif stage == 1:
            got(block, j, 1, 2, 3)
            parts = [from_z[block, j, slot] for slot in range(3)]
            ref[:, z_rows(z), :] = add(ref[:, z_rows(z), :], *parts).astype(BF)
            hand(block, j, 4, ref.at[ox, z_rows(z), :], from_x.at[block, j, 0:ROWS, :], to_x)
        else:
            got(block, j, 4)
            finish(block, j, add(ref[x, z_rows(z), :], from_x[block, j, 0:ROWS, :]))

    code_copy.wait_recv()
    attend(0, lambda chunk: None)
    loads[3].wait()

    def run_produce(block, after):
        for j in range(NJ):
            produce(block, j)
            if j >= 1:
                reduce_stage(0, block, j - 1)
            after(j)
        reduce_stage(0, block, NJ - 1)

    def serve(chunk):
        if chunk >= 4:
            reduce_stage(1, 0, chunk - 4)

    run_produce(0, lambda j: None)
    attend(1, serve)
    run_produce(1, lambda j: reduce_stage(2, 0, j))
    for j in range(NJ):
        reduce_stage(1, 1, j)
    for j in range(NJ):
        reduce_stage(2, 1, j)

    for which in range(2):
        for j in range(NJ):
            ref = out.at[:, pl.ds(which * HALF + j * JC, JC)]
            pltpu.make_async_copy(ref, ref, pp_recv.at[which * NJ + j]).wait()
    for copy in pending:
        copy.wait_send()


def local(
    input_codes,
    input_exps,
    prefix_len,
    norm_gain,
    w_query,
    w_keyval,
    w_out,
    kv_cache,
    partial_exps,
    share_exps,
    output_exps,
):
    half = np.power(np.float64(ROPE_BASE), -2.0 * np.arange(HD // 2) / HD).astype(np.float32)
    freqs = jnp.asarray(np.concatenate([half, half])[None, :])
    vmem = pl.BlockSpec(memory_space=pltpu.VMEM)
    smem = pl.BlockSpec(memory_space=pltpu.SMEM)
    hbm = pl.BlockSpec(memory_space=pl.ANY)
    dma = pltpu.SemaphoreType.DMA
    scratch = [
        pltpu.VMEM((NK, TOKENS, KC), BF),
        pltpu.VMEM((D, HEADS * HD), BF),
        pltpu.VMEM((D, 2 * HD), BF),
        pltpu.VMEM((HEADS * HD, D), BF),
        pltpu.VMEM((PREFIX, 2 * HD), BF),
        pltpu.VMEM((PREFIX, HD), BF),
        pltpu.VMEM((8, D), F32),
        pltpu.VMEM((TOKENS, (HEADS + 2) * HD), F32),
        pltpu.VMEM((TOKENS, HD), F32),
        pltpu.VMEM((TOKENS, HD), F32),
        pltpu.VMEM((2, HEADS * BLOCK, HD), BF),
        pltpu.VMEM((TOKENS, HD), BF),
        pltpu.VMEM((TOKENS, 2 * HD), BF),
        pltpu.VMEM((2, BLOCK, HEADS * HD), BF),
        pltpu.VMEM((2, NJ, BLOCK, JC), BF),
        pltpu.VMEM((2, NJ, BLOCK, JC), BF),
        pltpu.VMEM((2, NJ, 2, BLOCK // 2, JC), BF),
        pltpu.VMEM((2, NJ, BLOCK // 2, JC), BF),
        pltpu.VMEM((2, NJ, 3, 2, ROWS, JC), BF),
        pltpu.VMEM((2, NJ, ROWS, JC), BF),
        pltpu.VMEM((ROWS, HALF), BF),
        dma((4,)),
        dma((NK, 10)),
        dma((NK, 10)),
        dma((2 * NJ, 6)),
        dma((2 * NJ, 6)),
        dma((2,)),
        dma((2, NJ)),
        dma((2 * NJ,)),
    ]
    received = pl.pallas_call(
        kernel,
        out_shape=jax.ShapeDtypeStruct((ROWS, D), BF),
        in_specs=[vmem, smem, smem, vmem, vmem, hbm, hbm, hbm, hbm, smem, smem, smem],
        out_specs=hbm,
        scratch_shapes=scratch,
        compiler_params=pltpu.CompilerParams(
            collective_id=1, has_side_effects=True, vmem_limit_bytes=60 * 2**20
        ),
        cost_estimate=pl.CostEstimate(
            flops=10 * 10**9, bytes_accessed=26 * 2**20, transcendentals=9 * 10**6
        ),
        name="relay_section",
    )(
        input_codes[0],
        input_exps,
        prefix_len,
        norm_gain,
        freqs,
        w_query[0],
        w_keyval.reshape(D, 2 * HD),
        w_out[0],
        kv_cache.reshape(PREFIX, 2 * HD),
        partial_exps,
        share_exps,
        output_exps,
    )
    return received[None]


def solution(mesh):
    in_specs = (
        P("pp", "tp", None),
        P("pp", None),
        P("pp"),
        P("pp", None),
        P("pp", None, "tp"),
        P("pp", None, "tp", None),
        P("pp", "tp", None),
        P("pp", "tp", None, None),
        P("pp", None),
        P("pp", None),
        P(),
    )
    out_specs = P("pp", "tp", None)
    return jax.shard_map(local, mesh=mesh, in_specs=in_specs, out_specs=out_specs, check_vma=False)
```

```python
import functools
import math

import jax
import jax.numpy as jnp
import numpy as np
from jax import lax
from jax.experimental import pallas as pl
from jax.experimental.pallas import tpu as pltpu
from jax.sharding import PartitionSpec as P

EPSILON = 1e-05
ROPE_BASE = 500000.0
MESH = pl.DeviceIdType.MESH
BF = jnp.bfloat16
F32 = jnp.float32

SECTIONS = 8
D = 8192
HD = 128
HEADS = 4
ROWS = 16
BLOCK = 128
TOKENS = 256
PREFIX = 8192
LEAST = 2048
KC = 1024
NK = D // KC
HALF = D // 2
JC = 1024
NJ = HALF // JC
KEYS = 1024

Z_FIRST = "xxxxzzzz"
X_REDUCE = "xzxz"


def dot(a, b):
    return jnp.dot(a, b, preferred_element_type=F32)


def dot_t(a, b):
    return lax.dot_general(a, b, (((1,), (1,)), ((), ())), preferred_element_type=F32)


def token_of(row):
    return (((row % BLOCK) // ROWS) * 2 + row // BLOCK) * ROWS + row % ROWS


def kernel(
    codes_hbm,
    in_exps_hbm,
    prefix_hbm,
    gain_hbm,
    freqs_hbm,
    wq_hbm,
    wkv_hbm,
    wo_hbm,
    kv_hbm,
    part_exps_hbm,
    share_exps_hbm,
    out_exps_hbm,
    out,
    codes,
    in_exps,
    prefix_len,
    gain,
    freqs,
    part_exps,
    share_exps,
    out_exps,
    gathered,
    wq,
    wkv,
    wo,
    kv,
    keys,
    tables,
    acc,
    cosine,
    sine,
    queries,
    new_keys,
    new_values,
    attended,
    partial,
    from_sib,
    sums,
    from_x,
    from_z,
    outgoing,
    resid_codes,
    small_sem,
    load_sem,
    ag_send,
    ag_recv,
    rs_send,
    rs_recv,
    code_send_sem,
    code_recv_sem,
    pp_send,
    pp_recv,
):
    section = lax.axis_index("pp")
    rank = lax.axis_index("tp")
    core = rank % 2
    z = (rank // 2) % 4
    x = rank // 8
    other = 1 - core
    ox = 1 - x
    zn = (z + 1) % 4
    zp = (z + 3) % 4
    zo = (z + 2) % 4
    turned = (section % 4) // 3
    fx = (x + turned) % 2
    gx = 1 - fx
    came_x = (x + ((section + SECTIONS - 1) % 4) // 3) % 2

    def device(xx, zz, cc, steps=0):
        return {"pp": (section + steps) % SECTIONS, "tp": (xx * 4 + zz) * 2 + cc}

    to_next = device(x, zn, core)
    to_prev = device(x, zp, core)
    to_far = device(x, zo, core)
    to_x = device(ox, z, core)
    to_sib = device(x, z, other)

    small = [
        pltpu.make_async_copy(src, dst, small_sem.at[i])
        for i, (src, dst) in enumerate(
            (
                (codes_hbm, codes),
                (gain_hbm, gain),
                (in_exps_hbm, in_exps),
                (part_exps_hbm, part_exps),
                (share_exps_hbm, share_exps),
                (out_exps_hbm, out_exps),
                (prefix_hbm, prefix_len),
                (freqs_hbm, freqs),
            )
        )
    ]
    for load in small:
        load.start()
    barrier = pltpu.get_barrier_semaphore()
    greeted = [to_next, to_prev, to_far, to_x, to_sib, device(ox, z, other)]
    for cc in (core, other):
        greeted.append(device(came_x, z, cc, SECTIONS - 1))
    for peer in greeted:
        pl.semaphore_signal(barrier, inc=1, device_id=peer, device_id_type=MESH)

    loads = [
        pltpu.make_async_copy(src, dst, load_sem.at[i])
        for i, (src, dst) in enumerate(
            ((wq_hbm, wq), (wkv_hbm, wkv), (kv_hbm, kv), (wo_hbm, wo))
        )
    ]
    for load in loads:
        load.start()

    for load in small:
        load.wait()

    @pl.loop(0, D // HD // 8)
    def _(chunk):
        for inner in range(8):
            group = chunk * 8 + inner
            cols = pl.ds(pl.multiple_of(group * HD, HD), HD)

            def put(row, exponent):
                value = jnp.full((1, HD), jnp.left_shift(1, exponent + 16), jnp.int32)
                tables[row : row + 1, cols] = value.astype(F32) * (2.0**-16)

            part = part_exps[0, group]
            share = share_exps[0, group]
            outer = out_exps[section, group]
            put(0, in_exps[0, group])
            put(1, -part)
            put(2, part - share)
            put(3, share)
            put(4, -outer)
            put(5, outer)

    own_row = pl.multiple_of(core * BLOCK + (x * 4 + z) * ROWS, ROWS)
    power = jnp.zeros((ROWS, 1), F32)
    for k in range(NK):
        cols = slice(k * KC, (k + 1) * KC)
        resid = codes[:, cols].astype(F32) * tables[0:1, cols]
        power = power + jnp.sum(resid * resid, axis=1, keepdims=True)
    inverse = lax.rsqrt(power * (1.0 / D) + EPSILON)
    for k in range(NK):
        cols = slice(k * KC, (k + 1) * KC)
        resid = codes[:, cols].astype(F32) * tables[0:1, cols]
        gathered[k, pl.ds(own_row, ROWS), :] = (
            resid * inverse * gain[:, cols].astype(F32)
        ).astype(BF)

    pl.semaphore_wait(barrier, len(greeted))

    pending = []

    def remote(src, dst, send, recv, peer):
        copy = pltpu.make_async_remote_copy(
            src_ref=src,
            dst_ref=dst,
            send_sem=send,
            recv_sem=recv,
            device_id=peer,
            device_id_type=MESH,
        )
        copy.start()
        pending.append(copy)
        return copy

    def half_of(which):
        return pl.ds(pl.multiple_of(which * HALF, HALF), HALF)

    def code_send(which, peer):
        return pltpu.make_async_remote_copy(
            src_ref=codes.at[:, half_of(which)],
            dst_ref=resid_codes.at[core],
            send_sem=code_send_sem.at[which],
            recv_sem=code_recv_sem.at[core],
            device_id=peer,
            device_id_type=MESH,
        )

    def code_keep():
        return pltpu.make_async_copy(
            codes.at[:, half_of(core)], resid_codes.at[core], code_recv_sem.at[core]
        )

    def piece(xx, zz):
        return pl.ds(pl.multiple_of(core * BLOCK + (xx * 4 + zz) * ROWS, ROWS), ROWS)

    full = slice(0, KC)
    low = slice(0, KC // 2)
    high = slice(KC // 2, KC)
    copies = {}

    def share(k, slot, rows, cols, peer):
        ref = gathered.at[k, rows, cols]
        copies[k, slot] = remote(ref, ref, ag_send.at[k, slot], ag_recv.at[k, slot], peer)

    def arrived(k, *slots):
        for slot in slots:
            copies[k, slot].wait_recv()

    def x_rows(xx):
        return pl.ds(pl.multiple_of(core * BLOCK + xx * (BLOCK // 2), BLOCK // 2), BLOCK // 2)

    def gather_stage(stage, k):
        z_first = Z_FIRST[k] == "z"
        if stage == 0:
            share(k, 0, piece(x, z), full, to_x)
            share(k, 1, piece(x, z), full, to_next)
            share(k, 2, piece(x, z), full, to_prev)
        elif z_first and stage == 1:
            arrived(k, 1, 2)
            share(k, 3, piece(x, zp), low, to_next)
            share(k, 4, piece(x, zn), high, to_prev)
            share(k, 5, piece(x, zp), full, to_x)
            share(k, 6, piece(x, zn), full, to_x)
        elif z_first and stage == 2:
            arrived(k, 3, 4)
            share(k, 7, piece(x, zo), full, to_x)
            share(k, 8, x_rows(x), full, to_sib)
        elif z_first and stage == 3:
            arrived(k, 0, 5, 6, 7)
            share(k, 9, x_rows(ox), full, to_sib)
        elif z_first and stage == 4:
            arrived(k, 8, 9)
        elif stage == 1:
            arrived(k, 0)
            share(k, 3, piece(ox, z), full, to_next)
            share(k, 4, piece(ox, z), full, to_prev)
        elif stage == 2:
            arrived(k, 1, 2, 3, 4)
            share(k, 5, piece(x, zp), low, to_next)
            share(k, 6, piece(ox, zp), low, to_next)
            share(k, 7, piece(x, zn), high, to_prev)
            share(k, 8, piece(ox, zn), high, to_prev)
        elif stage == 3:
            arrived(k, 5, 6, 7, 8)
            rows = pl.ds(pl.multiple_of(core * BLOCK, BLOCK), BLOCK)
            share(k, 9, rows, full, to_sib)
        else:
            arrived(k, 9)

    def project(k):
        rows = gathered[k]
        cols = slice(k * KC, (k + 1) * KC)
        if k == 0:
            acc[:, : HEADS * HD] = dot(rows, wq[cols, :])
            acc[:, HEADS * HD :] = dot(rows, wkv[cols, :])
        else:
            acc[:, : HEADS * HD] += dot(rows, wq[cols, :])
            acc[:, HEADS * HD :] += dot(rows, wkv[cols, :])

    length = prefix_len[0]

    def make_rotary():
        row = lax.broadcasted_iota(jnp.int32, (TOKENS, HD), 0)
        angle = (length + token_of(row)).astype(F32) * freqs[...]
        lane = lax.broadcasted_iota(jnp.int32, (TOKENS, HD), 1)
        cosine[...] = jnp.cos(angle)
        sine[...] = jnp.where(lane < HD // 2, -1.0, 1.0) * jnp.sin(angle)

    def make_keys():
        first = kv[0:ROWS, :HD][0:1, :]

        @pl.loop(0, PREFIX // 1024)
        def _(chunk):
            start = pl.multiple_of(chunk * 1024, 1024)
            rows = pl.ds(start, 1024)
            position = lax.broadcasted_iota(jnp.int32, (1024, HD), 0) + start
            live = position < length
            keys[rows, :] = jnp.where(live, kv[rows, :HD], first)
            kv[rows, HD:] = jnp.where(live, kv[rows, HD:], jnp.zeros((), BF))
            kv[rows, :HD] = jnp.where(live, 1.0, 0.0).astype(BF)

    for k in range(NK):
        gather_stage(0, k)
    make_rotary()
    for k in range(NK // 2):
        gather_stage(1, k)
    loads[2].wait()
    make_keys()
    for k in range(NK // 2, NK):
        gather_stage(1, k)
        gather_stage(2, k - NK // 2)
    loads[0].wait()
    loads[1].wait()
    for k in range(NK // 2, NK):
        gather_stage(2, k)
        gather_stage(3, k - NK // 2)
    for k in range(NK // 2, NK + 1):
        if k < NK:
            gather_stage(3, k)
        gather_stage(4, k - NK // 2)
        project(k - NK // 2)
    for k in range(NK // 2 + 1, NK):
        gather_stage(4, k)
        project(k)

    @pl.when(turned == 1)
    def _():
        for which in range(2):
            code_send(which, device(ox, z, which)).start()

    @pl.when(turned == 0)
    def _():
        code_send(other, to_sib).start()
        code_keep().start()

    q_scale = math.log2(math.e) / math.sqrt(HD)

    def rotated(cols):
        value = acc[:, cols]
        return value * cosine[...] + pltpu.roll(value, HD // 2, 1) * sine[...]

    for head in range(HEADS):
        value = (rotated(slice(head * HD, (head + 1) * HD)) * q_scale).astype(BF)
        for block in range(2):
            queries[block, head * BLOCK : (head + 1) * BLOCK, :] = value[
                block * BLOCK : (block + 1) * BLOCK
            ]
    base = HEADS * HD
    new_keys[...] = rotated(slice(base, base + HD)).astype(BF)
    new_values[:, HD:] = acc[:, base + HD :].astype(BF)
    new_values[:, :HD] = jnp.ones((TOKENS, HD), BF)

    def attend(block, after):
        state = []
        row = lax.broadcasted_iota(jnp.int32, (BLOCK, TOKENS), 0) + block * BLOCK
        col = lax.broadcasted_iota(jnp.int32, (BLOCK, TOKENS), 1)
        seen = token_of(col) <= token_of(row)
        for head in range(HEADS):
            q = queries[block, head * BLOCK : (head + 1) * BLOCK, :]
            score = jnp.where(seen, dot_t(q, new_keys[...]), -1e30)
            top = jnp.max(score, axis=1, keepdims=True)
            weight = jnp.exp2(score - top).astype(BF)
            state.append((top, dot(weight, new_values[...])))
        for chunk in range(PREFIX // KEYS):
            rows = slice(chunk * KEYS, (chunk + 1) * KEYS)
            for head in range(HEADS):
                top, total = state[head]
                q = queries[block, head * BLOCK : (head + 1) * BLOCK, :]
                score = dot_t(q, keys[rows, :])
                new_top = jnp.maximum(top, jnp.max(score, axis=1, keepdims=True))
                weight = jnp.exp2(score - new_top).astype(BF)
                total = total * jnp.exp2(top - new_top) + dot(weight, kv[rows, :])
                state[head] = (new_top, total)
            after(chunk)
        for head in range(HEADS):
            total = state[head][1]
            attended[block, :, head * HD : (head + 1) * HD] = (
                total[:, HD:] / total[:, :HD]
            ).astype(BF)

    def half_cols(which, j):
        return pl.ds(pl.multiple_of(which * HALF + j * JC, JC), JC)

    def out_project(block, which, j):
        cols = half_cols(which, j)
        value = dot(attended[block], wo[:, cols]) * tables[1:2, cols]
        return jnp.clip(value, -127.0, 127.0).astype(BF)

    rs = {}

    def hand(block, j, slot, src, dst, peer):
        sem = block * NJ + j
        rs[block, j, slot] = remote(src, dst, rs_send.at[sem, slot], rs_recv.at[sem, slot], peer)

    def got(block, j, *slots):
        for slot in slots:
            rs[block, j, slot].wait_recv()

    def z_rows(zz):
        return pl.ds(pl.multiple_of(zz * ROWS, ROWS), ROWS)

    def add(*values):
        total = values[0].astype(F32)
        for value in values[1:]:
            total = total + value.astype(F32)
        return total

    def produce(block, j):
        partial[block, j] = out_project(block, other, j)
        hand(block, j, 0, partial.at[block, j], from_sib.at[block, j], to_sib)
        sums[block, j] = out_project(block, core, j).reshape(2, BLOCK // 2, JC)

    def finish(block, j, total):
        cols = half_cols(core, j)
        coded_in = resid_codes[block, :, j * JC : (j + 1) * JC]
        resid = coded_in.astype(F32) * tables[0:1, cols]
        codes4 = jnp.clip(total * tables[2:3, cols], -7.0, 7.0).astype(BF)
        updated = resid + codes4.astype(F32) * tables[3:4, cols]
        coded = jnp.clip(updated * tables[4:5, cols], -127.0, 127.0).astype(BF)
        outgoing[block, j] = (coded.astype(F32) * tables[5:6, cols]).astype(BF)
        slot = core * NJ + j
        remote(
            outgoing.at[block, j],
            out.at[:, cols],
            pp_send.at[block, j],
            pp_recv.at[slot],
            device(fx, z, block, 1),
        )

    across = ((0, zn, to_next), (1, zp, to_prev), (2, zo, to_far))

    def reduce_stage(stage, block, j):
        ref = sums.at[block, j]
        x_first = X_REDUCE[j] == "x"
        if stage == 0:
            got(block, j, 0)
            for part in range(2):
                rows = slice(part * (BLOCK // 2), (part + 1) * (BLOCK // 2))
                ref[part] = add(ref[part], from_sib[block, j, rows, :]).astype(BF)
            if x_first:
                hand(block, j, 1, ref.at[gx], from_x.at[block, j], to_x)
            else:
                for slot, zz, peer in across:
                    hand(block, j, 1 + slot, ref.at[:, z_rows(zz), :], from_z.at[block, j, slot], peer)
        elif x_first and stage == 1:
            got(block, j, 1)
            ref[fx] = add(ref[fx], from_x[block, j]).astype(BF)
            for slot, zz, peer in across:
                hand(block, j, 2 + slot, ref.at[fx, z_rows(zz), :], from_z.at[block, j, slot, 0], peer)
        elif x_first:
            got(block, j, 2, 3, 4)
            parts = [from_z[block, j, slot, 0] for slot in range(3)]
            finish(block, j, add(ref[fx, z_rows(z), :], *parts))
        elif stage == 1:
            got(block, j, 1, 2, 3)
            parts = [from_z[block, j, slot] for slot in range(3)]
            ref[:, z_rows(z), :] = add(ref[:, z_rows(z), :], *parts).astype(BF)
            hand(block, j, 4, ref.at[gx, z_rows(z), :], from_x.at[block, j, 0:ROWS, :], to_x)
        else:
            got(block, j, 4)
            finish(block, j, add(ref[fx, z_rows(z), :], from_x[block, j, 0:ROWS, :]))

    attend(0, lambda chunk: None)
    loads[3].wait()

    def run_produce(block, after):
        for j in range(NJ):
            produce(block, j)
            if j >= 1:
                reduce_stage(0, block, j - 1)
            after(j)
        reduce_stage(0, block, NJ - 1)

    def beside_attention(chunk):
        if chunk >= 6:
            reduce_stage(1, 0, chunk - 6)

    def beside_output(j):
        if j < 2:
            reduce_stage(1, 0, j + 2)
        else:
            reduce_stage(2, 0, j - 2)

    run_produce(0, lambda j: None)
    attend(1, beside_attention)
    for block in range(2):
        pltpu.make_async_copy(
            codes.at[:, half_of(0)], resid_codes.at[block], code_recv_sem.at[block]
        ).wait()
    run_produce(1, beside_output)
    reduce_stage(2, 0, 2)
    reduce_stage(2, 0, 3)
    for j in range(NJ):
        reduce_stage(1, 1, j)
    for j in range(NJ):
        reduce_stage(2, 1, j)

    for copy in pending:
        copy.wait_send()

    @pl.when(turned == 1)
    def _():
        for which in range(2):
            code_send(which, device(ox, z, which)).wait_send()

    @pl.when(turned == 0)
    def _():
        code_send(other, to_sib).wait_send()

    for which in range(2):
        for j in range(NJ):
            ref = out.at[:, pl.ds(which * HALF + j * JC, JC)]
            pltpu.make_async_copy(ref, ref, pp_recv.at[which * NJ + j]).wait()


def local(
    input_codes,
    input_exps,
    prefix_len,
    norm_gain,
    w_query,
    w_keyval,
    w_out,
    kv_cache,
    partial_exps,
    share_exps,
    output_exps,
):
    half = np.power(np.float64(ROPE_BASE), -2.0 * np.arange(HD // 2) / HD).astype(np.float32)
    freqs = jnp.asarray(np.concatenate([half, half])[None, :])
    hbm = pl.BlockSpec(memory_space=pl.ANY)
    dma = pltpu.SemaphoreType.DMA
    smem = pltpu.SMEM
    scratch = [
        pltpu.VMEM((ROWS, D), BF),
        smem((1, D // HD), jnp.int32),
        smem((1,), jnp.int32),
        pltpu.VMEM((1, D), BF),
        pltpu.VMEM((1, HD), F32),
        smem((1, D // HD), jnp.int32),
        smem((1, D // HD), jnp.int32),
        smem((SECTIONS, D // HD), jnp.int32),
        pltpu.VMEM((NK, TOKENS, KC), BF),
        pltpu.VMEM((D, HEADS * HD), BF),
        pltpu.VMEM((D, 2 * HD), BF),
        pltpu.VMEM((HEADS * HD, D), BF),
        pltpu.VMEM((PREFIX, 2 * HD), BF),
        pltpu.VMEM((PREFIX, HD), BF),
        pltpu.VMEM((8, D), F32),
        pltpu.VMEM((TOKENS, (HEADS + 2) * HD), F32),
        pltpu.VMEM((TOKENS, HD), F32),
        pltpu.VMEM((TOKENS, HD), F32),
        pltpu.VMEM((2, HEADS * BLOCK, HD), BF),
        pltpu.VMEM((TOKENS, HD), BF),
        pltpu.VMEM((TOKENS, 2 * HD), BF),
        pltpu.VMEM((2, BLOCK, HEADS * HD), BF),
        pltpu.VMEM((2, NJ, BLOCK, JC), BF),
        pltpu.VMEM((2, NJ, BLOCK, JC), BF),
        pltpu.VMEM((2, NJ, 2, BLOCK // 2, JC), BF),
        pltpu.VMEM((2, NJ, BLOCK // 2, JC), BF),
        pltpu.VMEM((2, NJ, 3, 2, ROWS, JC), BF),
        pltpu.VMEM((2, NJ, ROWS, JC), BF),
        pltpu.VMEM((2, ROWS, HALF), BF),
        dma((8,)),
        dma((4,)),
        dma((NK, 10)),
        dma((NK, 10)),
        dma((2 * NJ, 6)),
        dma((2 * NJ, 6)),
        dma((2,)),
        dma((2,)),
        dma((2, NJ)),
        dma((2 * NJ,)),
    ]
    received = pl.pallas_call(
        kernel,
        out_shape=jax.ShapeDtypeStruct((ROWS, D), BF),
        in_specs=[hbm] * 12,
        out_specs=hbm,
        scratch_shapes=scratch,
        compiler_params=pltpu.CompilerParams(
            collective_id=1, has_side_effects=True, vmem_limit_bytes=60 * 2**20
        ),
        cost_estimate=pl.CostEstimate(
            flops=10 * 10**9, bytes_accessed=26 * 2**20, transcendentals=9 * 10**6
        ),
        name="relay_section",
    )(
        input_codes[0],
        input_exps,
        prefix_len,
        norm_gain,
        freqs,
        w_query[0],
        w_keyval.reshape(D, 2 * HD),
        w_out[0],
        kv_cache.reshape(PREFIX, 2 * HD),
        partial_exps,
        share_exps,
        output_exps,
    )
    return received[None]


def solution(mesh):
    in_specs = (
        P("pp", "tp", None),
        P("pp", None),
        P("pp"),
        P("pp", None),
        P("pp", None, "tp"),
        P("pp", None, "tp", None),
        P("pp", "tp", None),
        P("pp", "tp", None, None),
        P("pp", None),
        P("pp", None),
        P(),
    )
    out_specs = P("pp", "tp", None)
    return jax.shard_map(local, mesh=mesh, in_specs=in_specs, out_specs=out_specs, check_vma=False)
```

```python
import functools
import math

import jax
import jax.numpy as jnp
import numpy as np
from jax import lax
from jax.experimental import pallas as pl
from jax.experimental.pallas import tpu as pltpu
from jax.sharding import PartitionSpec as P

EPSILON = 1e-05
ROPE_BASE = 500000.0
MESH = pl.DeviceIdType.MESH
BF = jnp.bfloat16
F32 = jnp.float32

SECTIONS = 8
D = 8192
HD = 128
HEADS = 4
ROWS = 16
BLOCK = 128
TOKENS = 256
PREFIX = 8192
LEAST = 2048
KC = 1024
NK = D // KC
HALF = D // 2
JC = 1024
NJ = HALF // JC
KEYS = 1024

Z_FIRST = "xxxxzzzz"
X_REDUCE = "xzxz"


def dot(a, b):
    return jnp.dot(a, b, preferred_element_type=F32)


def dot_t(a, b):
    return lax.dot_general(a, b, (((1,), (1,)), ((), ())), preferred_element_type=F32)


def token_of(row):
    return (((row % BLOCK) // ROWS) * 2 + row // BLOCK) * ROWS + row % ROWS


def kernel(
    codes_hbm,
    in_exps_hbm,
    prefix_hbm,
    gain,
    freqs_hbm,
    wq_hbm,
    wkv_hbm,
    wo_hbm,
    kv_hbm,
    part_exps_hbm,
    share_exps_hbm,
    out_exps_hbm,
    out,
    codes,
    in_exps,
    prefix_len,
    freqs,
    part_exps,
    share_exps,
    out_exps,
    gathered,
    wq,
    wkv,
    wo,
    kv,
    keys,
    tables,
    acc,
    cosine,
    sine,
    queries,
    new_keys,
    new_values,
    attended,
    partial,
    from_sib,
    sums,
    from_x,
    from_z,
    outgoing,
    resid_codes,
    small_sem,
    load_sem,
    ag_send,
    ag_recv,
    rs_send,
    rs_recv,
    code_send_sem,
    code_recv_sem,
    pp_send,
    pp_recv,
):
    section = lax.axis_index("pp")
    rank = lax.axis_index("tp")
    core = rank % 2
    z = (rank // 2) % 4
    x = rank // 8
    other = 1 - core
    ox = 1 - x
    zn = (z + 1) % 4
    zp = (z + 3) % 4
    zo = (z + 2) % 4
    turned = (section % 4) // 3
    fx = (x + turned) % 2
    gx = 1 - fx
    came_x = (x + ((section + SECTIONS - 1) % 4) // 3) % 2

    def device(xx, zz, cc, steps=0):
        return {"pp": (section + steps) % SECTIONS, "tp": (xx * 4 + zz) * 2 + cc}

    to_next = device(x, zn, core)
    to_prev = device(x, zp, core)
    to_far = device(x, zo, core)
    to_x = device(ox, z, core)
    to_sib = device(x, z, other)

    small = [
        pltpu.make_async_copy(src, dst, small_sem.at[i])
        for i, (src, dst) in enumerate(
            (
                (codes_hbm, codes),
                (in_exps_hbm, in_exps),
                (part_exps_hbm, part_exps),
                (share_exps_hbm, share_exps),
                (out_exps_hbm, out_exps),
                (prefix_hbm, prefix_len),
                (freqs_hbm, freqs),
            )
        )
    ]
    for load in small:
        load.start()
    barrier = pltpu.get_barrier_semaphore()
    greeted = [to_next, to_prev, to_far, to_x, to_sib, device(ox, z, other)]
    for cc in (core, other):
        greeted.append(device(came_x, z, cc, SECTIONS - 1))
    for peer in greeted:
        pl.semaphore_signal(barrier, inc=1, device_id=peer, device_id_type=MESH)

    loads = [
        pltpu.make_async_copy(src, dst, load_sem.at[i])
        for i, (src, dst) in enumerate(
            ((wq_hbm, wq), (wkv_hbm, wkv), (kv_hbm, kv), (wo_hbm, wo))
        )
    ]
    for load in loads:
        load.start()

    for load in small:
        load.wait()

    @pl.loop(0, D // HD // 8)
    def _(chunk):
        for inner in range(8):
            group = chunk * 8 + inner
            cols = pl.ds(pl.multiple_of(group * HD, HD), HD)

            def put(row, exponent):
                value = jnp.full((1, HD), jnp.left_shift(1, exponent + 16), jnp.int32)
                tables[row : row + 1, cols] = value.astype(F32) * (2.0**-16)

            part = part_exps[0, group]
            share = share_exps[0, group]
            outer = out_exps[section, group]
            put(0, in_exps[0, group])
            put(1, -part)
            put(2, part - share)
            put(3, share)
            put(4, -outer)
            put(5, outer)

    own_row = pl.multiple_of(core * BLOCK + (x * 4 + z) * ROWS, ROWS)
    power = jnp.zeros((ROWS, 1), F32)
    for k in range(NK):
        cols = slice(k * KC, (k + 1) * KC)
        resid = codes[:, cols].astype(F32) * tables[0:1, cols]
        power = power + jnp.sum(resid * resid, axis=1, keepdims=True)
    inverse = lax.rsqrt(power * (1.0 / D) + EPSILON)
    for k in range(NK):
        cols = slice(k * KC, (k + 1) * KC)
        resid = codes[:, cols].astype(F32) * tables[0:1, cols]
        gathered[k, pl.ds(own_row, ROWS), :] = (
            resid * inverse * gain[:, cols].astype(F32)
        ).astype(BF)

    pl.semaphore_wait(barrier, len(greeted))

    pending = []

    def remote(src, dst, send, recv, peer):
        copy = pltpu.make_async_remote_copy(
            src_ref=src,
            dst_ref=dst,
            send_sem=send,
            recv_sem=recv,
            device_id=peer,
            device_id_type=MESH,
        )
        copy.start()
        pending.append(copy)
        return copy

    def half_of(which):
        return pl.ds(pl.multiple_of(which * HALF, HALF), HALF)

    def code_send(which, peer):
        return pltpu.make_async_remote_copy(
            src_ref=codes.at[:, half_of(which)],
            dst_ref=resid_codes.at[core],
            send_sem=code_send_sem.at[which],
            recv_sem=code_recv_sem.at[core],
            device_id=peer,
            device_id_type=MESH,
        )

    def code_keep():
        return pltpu.make_async_copy(
            codes.at[:, half_of(core)], resid_codes.at[core], code_recv_sem.at[core]
        )

    def piece(xx, zz):
        return pl.ds(pl.multiple_of(core * BLOCK + (xx * 4 + zz) * ROWS, ROWS), ROWS)

    full = slice(0, KC)
    low = slice(0, KC // 2)
    high = slice(KC // 2, KC)
    copies = {}

    def share(k, slot, rows, cols, peer):
        ref = gathered.at[k, rows, cols]
        copies[k, slot] = remote(ref, ref, ag_send.at[k, slot], ag_recv.at[k, slot], peer)

    def arrived(k, *slots):
        for slot in slots:
            copies[k, slot].wait_recv()

    def x_rows(xx):
        return pl.ds(pl.multiple_of(core * BLOCK + xx * (BLOCK // 2), BLOCK // 2), BLOCK // 2)

    def gather_stage(stage, k):
        z_first = Z_FIRST[k] == "z"
        if stage == 0:
            share(k, 0, piece(x, z), full, to_x)
            share(k, 1, piece(x, z), full, to_next)
            share(k, 2, piece(x, z), full, to_prev)
        elif z_first and stage == 1:
            arrived(k, 1, 2)
            share(k, 3, piece(x, zp), low, to_next)
            share(k, 4, piece(x, zn), high, to_prev)
            share(k, 5, piece(x, zp), full, to_x)
            share(k, 6, piece(x, zn), full, to_x)
        elif z_first and stage == 2:
            arrived(k, 3, 4)
            share(k, 7, piece(x, zo), full, to_x)
            share(k, 8, x_rows(x), full, to_sib)
        elif z_first and stage == 3:
            arrived(k, 0, 5, 6, 7)
            share(k, 9, x_rows(ox), full, to_sib)
        elif z_first and stage == 4:
            arrived(k, 8, 9)
        elif stage == 1:
            arrived(k, 0)
            share(k, 3, piece(ox, z), full, to_next)
            share(k, 4, piece(ox, z), full, to_prev)
        elif stage == 2:
            arrived(k, 1, 2, 3, 4)
            share(k, 5, piece(x, zp), low, to_next)
            share(k, 6, piece(ox, zp), low, to_next)
            share(k, 7, piece(x, zn), high, to_prev)
            share(k, 8, piece(ox, zn), high, to_prev)
        elif stage == 3:
            arrived(k, 5, 6, 7, 8)
            rows = pl.ds(pl.multiple_of(core * BLOCK, BLOCK), BLOCK)
            share(k, 9, rows, full, to_sib)
        else:
            arrived(k, 9)

    def project(k):
        rows = gathered[k]
        cols = slice(k * KC, (k + 1) * KC)
        if k == 0:
            acc[:, : HEADS * HD] = dot(rows, wq[cols, :])
            acc[:, HEADS * HD :] = dot(rows, wkv[cols, :])
        else:
            acc[:, : HEADS * HD] += dot(rows, wq[cols, :])
            acc[:, HEADS * HD :] += dot(rows, wkv[cols, :])

    length = prefix_len[0]

    def make_rotary():
        row = lax.broadcasted_iota(jnp.int32, (TOKENS, HD), 0)
        angle = (length + token_of(row)).astype(F32) * freqs[...]
        lane = lax.broadcasted_iota(jnp.int32, (TOKENS, HD), 1)
        cosine[...] = jnp.cos(angle)
        sine[...] = jnp.where(lane < HD // 2, -1.0, 1.0) * jnp.sin(angle)

    def make_keys():
        first = kv[0:ROWS, :HD][0:1, :]

        @pl.loop(0, PREFIX // 1024)
        def _(chunk):
            start = pl.multiple_of(chunk * 1024, 1024)
            rows = pl.ds(start, 1024)
            position = lax.broadcasted_iota(jnp.int32, (1024, HD), 0) + start
            live = position < length
            keys[rows, :] = jnp.where(live, kv[rows, :HD], first)
            kv[rows, HD:] = jnp.where(live, kv[rows, HD:], jnp.zeros((), BF))
            kv[rows, :HD] = jnp.where(live, 1.0, 0.0).astype(BF)

    for k in range(NK):
        gather_stage(0, k)
    make_rotary()
    for k in range(NK // 2):
        gather_stage(1, k)
    loads[2].wait()
    make_keys()
    for k in range(NK // 2, NK):
        gather_stage(1, k)
        gather_stage(2, k - NK // 2)
    loads[0].wait()
    loads[1].wait()
    for k in range(NK // 2, NK):
        gather_stage(2, k)
        gather_stage(3, k - NK // 2)
    for k in range(NK // 2, NK + 1):
        if k < NK:
            gather_stage(3, k)
        gather_stage(4, k - NK // 2)
        project(k - NK // 2)
    for k in range(NK // 2 + 1, NK):
        gather_stage(4, k)
        project(k)

    @pl.when(turned == 1)
    def _():
        for which in range(2):
            code_send(which, device(ox, z, which)).start()

    @pl.when(turned == 0)
    def _():
        code_send(other, to_sib).start()
        code_keep().start()

    q_scale = math.log2(math.e) / math.sqrt(HD)

    def rotated(cols):
        value = acc[:, cols]
        return value * cosine[...] + pltpu.roll(value, HD // 2, 1) * sine[...]

    for head in range(HEADS):
        value = (rotated(slice(head * HD, (head + 1) * HD)) * q_scale).astype(BF)
        for block in range(2):
            queries[block, head * BLOCK : (head + 1) * BLOCK, :] = value[
                block * BLOCK : (block + 1) * BLOCK
            ]
    base = HEADS * HD
    new_keys[...] = rotated(slice(base, base + HD)).astype(BF)
    new_values[:, HD:] = acc[:, base + HD :].astype(BF)
    new_values[:, :HD] = jnp.ones((TOKENS, HD), BF)

    def attend(block, after):
        state = []
        row = lax.broadcasted_iota(jnp.int32, (BLOCK, TOKENS), 0) + block * BLOCK
        col = lax.broadcasted_iota(jnp.int32, (BLOCK, TOKENS), 1)
        seen = token_of(col) <= token_of(row)
        for head in range(HEADS):
            q = queries[block, head * BLOCK : (head + 1) * BLOCK, :]
            score = jnp.where(seen, dot_t(q, new_keys[...]), -1e30)
            top = jnp.max(score, axis=1, keepdims=True)
            weight = jnp.exp2(score - top).astype(BF)
            state.append((top, dot(weight, new_values[...])))
        for chunk in range(PREFIX // KEYS):
            rows = slice(chunk * KEYS, (chunk + 1) * KEYS)
            for head in range(HEADS):
                top, total = state[head]
                q = queries[block, head * BLOCK : (head + 1) * BLOCK, :]
                score = dot_t(q, keys[rows, :])
                new_top = jnp.maximum(top, jnp.max(score, axis=1, keepdims=True))
                weight = jnp.exp2(score - new_top).astype(BF)
                total = total * jnp.exp2(top - new_top) + dot(weight, kv[rows, :])
                state[head] = (new_top, total)
            after(chunk)
        for head in range(HEADS):
            total = state[head][1]
            attended[block, :, head * HD : (head + 1) * HD] = (
                total[:, HD:] / total[:, :HD]
            ).astype(BF)

    def half_cols(which, j):
        return pl.ds(pl.multiple_of(which * HALF + j * JC, JC), JC)

    def out_project(block, which, j):
        cols = half_cols(which, j)
        value = dot(attended[block], wo[:, cols]) * tables[1:2, cols]
        return jnp.clip(value, -127.0, 127.0).astype(BF)

    rs = {}

    def hand(block, j, slot, src, dst, peer):
        sem = block * NJ + j
        rs[block, j, slot] = remote(src, dst, rs_send.at[sem, slot], rs_recv.at[sem, slot], peer)

    def got(block, j, *slots):
        for slot in slots:
            rs[block, j, slot].wait_recv()

    def z_rows(zz):
        return pl.ds(pl.multiple_of(zz * ROWS, ROWS), ROWS)

    def add(*values):
        total = values[0].astype(F32)
        for value in values[1:]:
            total = total + value.astype(F32)
        return total

    def produce(block, j):
        partial[block, j] = out_project(block, other, j)
        hand(block, j, 0, partial.at[block, j], from_sib.at[block, j], to_sib)
        sums[block, j] = out_project(block, core, j).reshape(2, BLOCK // 2, JC)

    def finish(block, j, total):
        cols = half_cols(core, j)
        coded_in = resid_codes[block, :, j * JC : (j + 1) * JC]
        resid = coded_in.astype(F32) * tables[0:1, cols]
        codes4 = jnp.clip(total * tables[2:3, cols], -7.0, 7.0).astype(BF)
        updated = resid + codes4.astype(F32) * tables[3:4, cols]
        coded = jnp.clip(updated * tables[4:5, cols], -127.0, 127.0).astype(BF)
        outgoing[block, j] = (coded.astype(F32) * tables[5:6, cols]).astype(BF)
        slot = core * NJ + j
        remote(
            outgoing.at[block, j],
            out.at[:, cols],
            pp_send.at[block, j],
            pp_recv.at[slot],
            device(fx, z, block, 1),
        )

    across = ((0, zn, to_next), (1, zp, to_prev), (2, zo, to_far))

    def reduce_stage(stage, block, j):
        ref = sums.at[block, j]
        x_first = X_REDUCE[j] == "x"
        if stage == 0:
            got(block, j, 0)
            for part in range(2):
                rows = slice(part * (BLOCK // 2), (part + 1) * (BLOCK // 2))
                ref[part] = add(ref[part], from_sib[block, j, rows, :]).astype(BF)
            if x_first:
                hand(block, j, 1, ref.at[gx], from_x.at[block, j], to_x)
            else:
                for slot, zz, peer in across:
                    hand(block, j, 1 + slot, ref.at[:, z_rows(zz), :], from_z.at[block, j, slot], peer)
        elif x_first and stage == 1:
            got(block, j, 1)
            ref[fx] = add(ref[fx], from_x[block, j]).astype(BF)
            for slot, zz, peer in across:
                hand(block, j, 2 + slot, ref.at[fx, z_rows(zz), :], from_z.at[block, j, slot, 0], peer)
        elif x_first:
            got(block, j, 2, 3, 4)
            parts = [from_z[block, j, slot, 0] for slot in range(3)]
            finish(block, j, add(ref[fx, z_rows(z), :], *parts))
        elif stage == 1:
            got(block, j, 1, 2, 3)
            parts = [from_z[block, j, slot] for slot in range(3)]
            ref[:, z_rows(z), :] = add(ref[:, z_rows(z), :], *parts).astype(BF)
            hand(block, j, 4, ref.at[gx, z_rows(z), :], from_x.at[block, j, 0:ROWS, :], to_x)
        else:
            got(block, j, 4)
            finish(block, j, add(ref[fx, z_rows(z), :], from_x[block, j, 0:ROWS, :]))

    attend(0, lambda chunk: None)
    loads[3].wait()

    def run_produce(block, after):
        for j in range(NJ):
            produce(block, j)
            if j >= 1:
                reduce_stage(0, block, j - 1)
            after(j)
        reduce_stage(0, block, NJ - 1)

    def beside_attention(chunk):
        if chunk >= 6:
            reduce_stage(1, 0, chunk - 6)

    def beside_output(j):
        if j < 2:
            reduce_stage(1, 0, j + 2)
        else:
            reduce_stage(2, 0, j - 2)

    run_produce(0, lambda j: None)
    attend(1, beside_attention)
    for block in range(2):
        pltpu.make_async_copy(
            codes.at[:, half_of(0)], resid_codes.at[block], code_recv_sem.at[block]
        ).wait()
    run_produce(1, beside_output)
    reduce_stage(2, 0, 2)
    reduce_stage(2, 0, 3)
    for j in range(NJ):
        reduce_stage(1, 1, j)
    for j in range(NJ):
        reduce_stage(2, 1, j)

    for copy in pending:
        copy.wait_send()

    @pl.when(turned == 1)
    def _():
        for which in range(2):
            code_send(which, device(ox, z, which)).wait_send()

    @pl.when(turned == 0)
    def _():
        code_send(other, to_sib).wait_send()

    for which in range(2):
        for j in range(NJ):
            ref = out.at[:, pl.ds(which * HALF + j * JC, JC)]
            pltpu.make_async_copy(ref, ref, pp_recv.at[which * NJ + j]).wait()


def local(
    input_codes,
    input_exps,
    prefix_len,
    norm_gain,
    w_query,
    w_keyval,
    w_out,
    kv_cache,
    partial_exps,
    share_exps,
    output_exps,
):
    half = np.power(np.float64(ROPE_BASE), -2.0 * np.arange(HD // 2) / HD).astype(np.float32)
    freqs = jnp.asarray(np.concatenate([half, half])[None, :])
    vmem = pl.BlockSpec(memory_space=pltpu.VMEM)
    hbm = pl.BlockSpec(memory_space=pl.ANY)
    dma = pltpu.SemaphoreType.DMA
    smem = pltpu.SMEM
    scratch = [
        pltpu.VMEM((ROWS, D), BF),
        smem((1, D // HD), jnp.int32),
        smem((1,), jnp.int32),
        pltpu.VMEM((1, HD), F32),
        smem((1, D // HD), jnp.int32),
        smem((1, D // HD), jnp.int32),
        smem((SECTIONS, D // HD), jnp.int32),
        pltpu.VMEM((NK, TOKENS, KC), BF),
        pltpu.VMEM((D, HEADS * HD), BF),
        pltpu.VMEM((D, 2 * HD), BF),
        pltpu.VMEM((HEADS * HD, D), BF),
        pltpu.VMEM((PREFIX, 2 * HD), BF),
        pltpu.VMEM((PREFIX, HD), BF),
        pltpu.VMEM((8, D), F32),
        pltpu.VMEM((TOKENS, (HEADS + 2) * HD), F32),
        pltpu.VMEM((TOKENS, HD), F32),
        pltpu.VMEM((TOKENS, HD), F32),
        pltpu.VMEM((2, HEADS * BLOCK, HD), BF),
        pltpu.VMEM((TOKENS, HD), BF),
        pltpu.VMEM((TOKENS, 2 * HD), BF),
        pltpu.VMEM((2, BLOCK, HEADS * HD), BF),
        pltpu.VMEM((2, NJ, BLOCK, JC), BF),
        pltpu.VMEM((2, NJ, BLOCK, JC), BF),
        pltpu.VMEM((2, NJ, 2, BLOCK // 2, JC), BF),
        pltpu.VMEM((2, NJ, BLOCK // 2, JC), BF),
        pltpu.VMEM((2, NJ, 3, 2, ROWS, JC), BF),
        pltpu.VMEM((2, NJ, ROWS, JC), BF),
        pltpu.VMEM((2, ROWS, HALF), BF),
        dma((7,)),
        dma((4,)),
        dma((NK, 10)),
        dma((NK, 10)),
        dma((2 * NJ, 6)),
        dma((2 * NJ, 6)),
        dma((2,)),
        dma((2,)),
        dma((2, NJ)),
        dma((2 * NJ,)),
    ]
    received = pl.pallas_call(
        kernel,
        out_shape=jax.ShapeDtypeStruct((ROWS, D), BF),
        in_specs=[hbm] * 3 + [vmem] + [hbm] * 8,
        out_specs=hbm,
        scratch_shapes=scratch,
        compiler_params=pltpu.CompilerParams(
            collective_id=1, has_side_effects=True, vmem_limit_bytes=60 * 2**20
        ),
        cost_estimate=pl.CostEstimate(
            flops=10 * 10**9, bytes_accessed=26 * 2**20, transcendentals=9 * 10**6
        ),
        name="relay_section",
    )(
        input_codes[0],
        input_exps,
        prefix_len,
        norm_gain,
        freqs,
        w_query[0],
        w_keyval.reshape(D, 2 * HD),
        w_out[0],
        kv_cache.reshape(PREFIX, 2 * HD),
        partial_exps,
        share_exps,
        output_exps,
    )
    return received[None]


def solution(mesh):
    in_specs = (
        P("pp", "tp", None),
        P("pp", None),
        P("pp"),
        P("pp", None),
        P("pp", None, "tp"),
        P("pp", None, "tp", None),
        P("pp", "tp", None),
        P("pp", "tp", None, None),
        P("pp", None),
        P("pp", None),
        P(),
    )
    out_specs = P("pp", "tp", None)
    return jax.shard_map(local, mesh=mesh, in_specs=in_specs, out_specs=out_specs, check_vma=False)
```
